512 devices in a mesh: freq: 8 (over z), src: 64 (over y, x, core).
Axes of the slice: x: 4, y: 8, z: 8, core: 2. Of those that a mesh axis runs over, the one named last changes fastest.
Arguments:
- downgoing: float32 [16, 2048, 16384], P('freq', None, 'src'), parts along dimension 0, may hold values from -0.234375 to 0.234375
- upgoing: float32 [16, 16384, 128], P('freq', 'src'), parts along dimension 0, may hold values from -6 to 6
Outputs:
- reflectivity: float32 [2048, 16, 128], P('src', 'freq'), parts along dimension 1
- residual: float32 [16, 16384, 128], P('freq', 'src'), parts along dimension 0
The draws below stay inside these ranges and needn't reach their ends.
There are 8 independent parts, one for each index of `freq`. The reference program is written for one: setup_inputs(seed, part) draws one part's arguments, and reference() takes and returns one part's arrays. A program takes and returns all parts, laid end to end along the dimension named above; each array names one. Nothing has to cross between parts.
All inputs are finite; a program needn't handle non-finite values.
Results may differ from the reference program's by a relative error of at most 0.0003.
Values sent between devices are 32-bit elements; how exact they have to be, the bound alone decides.
No kernel may reach another device: no remote copies, remote signals or barrier semaphores. Data moves between devices by JAX's collectives and lax.ppermute only.
A program may use at most 64 MiB of HBM per device.

```python
import math
import jax
import jax.numpy as jnp
from jax import lax

R = 2048
V = 128
ITERS = 2
SOURCES = 16384


def draw_downgoing(key, part):
    key = jax.random.fold_in(key, 11)
    key_a, key_b, key_c = jax.random.split(key, 3)
    entries = jnp.clip(jax.random.normal(key_a, (2, R, SOURCES), jnp.float32), -4.0, 4.0)
    row_scale = jnp.exp(jax.random.uniform(key_b, (R, 1), jnp.float32, math.log(0.3), math.log(3.0)))
    ramp = jnp.arange(SOURCES, dtype=jnp.float32) / SOURCES
    col_scale = jnp.exp(math.log(3.0) * ramp + jax.random.uniform(key_c, (SOURCES,), jnp.float32, 0.0, math.log(3.3)))
    return entries * row_scale * col_scale / (4.0 * math.sqrt(SOURCES))


def shard_levels(rng, dims, shards, least, largest):
    factor_of, own = 1.0, jax.random.fold_in(rng, 6)
    for dim, parts in shards:
        steps = jnp.exp(jax.random.uniform(jax.random.fold_in(own, dim), (parts,), jnp.float32, least / len(shards), largest / len(shards)))
        factor_of = factor_of * jnp.repeat(steps, dims[dim] // parts).reshape([-1 if axis == dim else 1 for axis in range(len(dims))])
    return factor_of


def normal_values(stream_key, extent, width, limit, pieces=(), kind=jnp.bfloat16):
    values = jax.random.normal(stream_key, extent, jnp.float32) * width
    if len(pieces) > 0:
        values = shard_levels(stream_key, extent, pieces, -0.22, 0.18) * values
    return jnp.clip(values, min=-limit, max=limit).astype(kind)


def setup_inputs(seed: int = 0, part: int = 0) -> dict:
    keys = jax.random.split(jax.random.key(seed), 3)
    part_keys = jax.random.split(jax.random.fold_in(keys[2], part), 3)
    return {
        "downgoing": draw_downgoing(jax.random.fold_in(jax.random.fold_in(keys[2], part), 71), part),
        "upgoing": normal_values(part_keys[1], (2, SOURCES, V), 1.0, 6.0, ((1, 64),), jnp.float32),
    }


HI = lax.Precision.HIGHEST


def contract_first(a, b):
    return lax.dot_general(a, b, (((0,), (0,)), ((), ())), precision=HI, preferred_element_type=jnp.float32)


def adjoint(downgoing, residual):
    real = jnp.dot(downgoing[0], residual[0], precision=HI, preferred_element_type=jnp.float32) + jnp.dot(downgoing[1], residual[1], precision=HI, preferred_element_type=jnp.float32)
    imag = jnp.dot(downgoing[0], residual[1], precision=HI, preferred_element_type=jnp.float32) - jnp.dot(downgoing[1], residual[0], precision=HI, preferred_element_type=jnp.float32)
    return jnp.stack([real, imag], axis=1)


def forward(downgoing, direction):
    real = contract_first(downgoing[0], direction[:, 0]) - contract_first(downgoing[1], direction[:, 1])
    imag = contract_first(downgoing[0], direction[:, 1]) + contract_first(downgoing[1], direction[:, 0])
    return jnp.stack([real, imag])


def reference(downgoing, upgoing):
    residual = upgoing
    filt = jnp.zeros((R, 2, V), jnp.float32)
    direction = jnp.zeros((R, 2, V), jnp.float32)
    gamma = jnp.float32(1.0)
    for step in range(ITERS):
        gradient = adjoint(downgoing, residual)
        gamma_new = jnp.sum(gradient * gradient)
        if step == 0:
            direction = gradient
        else:
            direction = gradient + (gamma_new / gamma) * direction
        gamma = gamma_new
        image = forward(downgoing, direction)
        alpha = gamma / jnp.sum(image * image)
        filt = filt + alpha * direction
        residual = residual - alpha * image
    return filt, residual
```

```python
import jax
import jax.numpy as jnp
from jax import lax
from jax.sharding import PartitionSpec as P

HI = lax.Precision.HIGH
CHIPS = 32
SAME_CORE = [[2 * j + c for j in range(CHIPS)] for c in range(2)]
SWAP = [(i, i ^ 1) for i in range(2 * CHIPS)]


def dot(a, b, dims):
    return lax.dot_general(a, b, ((dims[0], dims[1]), ((), ())), precision=HI, preferred_element_type=jnp.float32)


def exchange(blocks):
    return lax.all_to_all(blocks, "src", 0, 0, axis_index_groups=SAME_CORE, tiled=True)


def pack(re, im):
    return jnp.concatenate([re[:, :64], im[:, :64]], 1), jnp.concatenate([re[:, 64:], im[:, 64:]], 1)


def turn(z):
    return jnp.concatenate([-z[:, 64:], z[:, :64]], 1)


def adjoint(down, field):
    return dot(down[0], field, ((1,), (0,))) - dot(down[1], turn(field), ((1,), (0,)))


def forward(down, piece):
    return dot(down[0], piece, ((0,), (0,))) + dot(down[1], turn(piece), ((0,), (0,)))


def all_sum(partial):
    rows = partial.shape[0]
    parts = exchange(partial.reshape(CHIPS, rows // CHIPS, 128))
    block = jnp.sum(parts, axis=0)
    return exchange(jnp.broadcast_to(block, parts.shape)).reshape(rows, 128)


def ratio(a, b, other):
    good = b > 0
    return jnp.where(good, a / jnp.where(good, b, 1.0), other)


def on_device(downgoing, upgoing):
    core = lax.axis_index("src") % 2
    chip = lax.axis_index("src") // 2
    lower = core == 0
    low, high = pack(upgoing[0], upgoing[1])
    mine, theirs = jnp.where(lower, low, high), jnp.where(lower, high, low)
    both = adjoint(downgoing, mine), adjoint(downgoing, theirs)
    partial = both[0] + lax.ppermute(both[1], "src", SWAP)
    other_down = lax.ppermute(downgoing, "src", SWAP)
    g0 = all_sum(partial)

    image0_own, image0_other = forward(downgoing, g0), forward(other_down, g0)
    q = all_sum(adjoint(downgoing, image0_own) + adjoint(other_down, image0_other))

    gamma0 = jnp.sum(g0 * g0)
    m1 = jnp.sum(g0 * q)
    a = ratio(gamma0, m1, 1.0)
    g1 = g0 - a * q
    gamma1 = jnp.sum(g1 * g1)
    beta = ratio(gamma1, gamma0, 0.0)
    p1 = g1 + beta * g0
    image1_own, image1_other = forward(downgoing, p1), forward(other_down, p1)
    square = jnp.sum(image1_own * image1_own) + jnp.sum(image1_other * image1_other)

    lane = lax.broadcasted_iota(jnp.int32, (2 * CHIPS, 8, 128), 2)
    row = jnp.where(lane == 0, square, jnp.where(lane == 1, gamma0, jnp.where(lane == 2, m1, gamma1)))
    got = lax.all_to_all(row, "src", 0, 0, tiled=True)[:, 0]
    sq = jnp.sum(got[:, 0].reshape(CHIPS, 2), axis=0)
    ga0, m, ga1 = got[:2, 1], got[:2, 2], got[:2, 3]

    ac = ratio(ga0, m, 1.0)
    bc = ratio(ga1, ga0, 0.0)
    gamma = jnp.sum(ga0)
    alpha0 = gamma / jnp.sum(m)
    s = alpha0 / ac
    gamma_new = jnp.sum(s * s * ga1 + (1.0 - s) * (1.0 - s) * ga0)
    e = gamma_new / gamma + 1.0 - s - s * bc
    alpha1 = gamma_new / jnp.sum(s * s * sq + e * e * m)
    k0 = alpha0 + alpha1 * e
    k1 = alpha1 * s

    def halves(k):
        return jnp.where(lower, k[0], k[1]), jnp.where(lower, k[1], k[0])

    mine0, theirs0 = halves(k0)
    mine1, theirs1 = halves(k1)

    def rows32(z, which):
        return lax.dynamic_slice_in_dim(z, chip * 64 + 32 * which, 32, 0)

    give = jnp.concatenate([image0_other, image1_other, rows32(g0, 1 - core), rows32(p1, 1 - core)], 0)
    take = lax.ppermute(give, "src", SWAP)
    image0_take, image1_take, g0_take, p1_take = take[:256], take[256:512], take[512:544], take[544:]

    def out(mine, theirs):
        low, high = jnp.where(lower, mine, theirs), jnp.where(lower, theirs, mine)
        return jnp.concatenate([low[:, :64], high[:, :64]], 1), jnp.concatenate([low[:, 64:], high[:, 64:]], 1)

    res_mine = mine - mine0 * image0_own - mine1 * image1_own
    res_theirs = theirs - theirs0 * image0_take - theirs1 * image1_take
    residual = jnp.stack(out(res_mine, res_theirs))
    filt = jnp.stack(
        out(mine0 * rows32(g0, core) + mine1 * rows32(p1, core), theirs0 * g0_take + theirs1 * p1_take), axis=1
    )
    return (filt, residual)


def solution(mesh):
    placed = (P("freq", None, "src"), P("freq", "src", None))
    return jax.shard_map(
        on_device,
        mesh=mesh,
        in_specs=placed,
        out_specs=(P("src", "freq", None), P("freq", "src", None)),
        check_vma=False,
    )
```

```python
import functools

import jax
import jax.numpy as jnp
from jax import lax
from jax.experimental import pallas as pl
from jax.experimental.pallas import tpu as pltpu
from jax.sharding import Mesh, PartitionSpec as P

SRC = ("y", "x", "core")
CHIPS = 32
ROWS = 2048
OWN = 256
STEP = 256
STEPS = ROWS // STEP
SWAP = [(i, i ^ 1) for i in range(2 * CHIPS)]
VMEM = pl.BlockSpec(memory_space=pltpu.VMEM)
SMEM = pl.BlockSpec(memory_space=pltpu.SMEM)
PARAMS = pltpu.CompilerParams(vmem_limit_bytes=56 * 2**20)
F32 = jnp.float32
BF16 = jnp.bfloat16


def dot(a, b):
    return jnp.dot(a, b, preferred_element_type=F32)


def split(x):
    high = x.astype(BF16)
    return high, (x - high.astype(F32)).astype(BF16)


def lanes(x):
    return lax.broadcasted_iota(jnp.int32, x.shape, x.ndim - 1) < 64


def turn(z):
    swapped = pltpu.roll(z, 64, 1)
    return jnp.where(lanes(z), -swapped, swapped)


def halves(re, im):
    first = lanes(re)
    return jnp.where(first, re, pltpu.roll(im, 64, 1)), jnp.where(first, pltpu.roll(re, 64, 1), im)


def ratio(a, b, other):
    good = b > 0
    return jnp.where(good, a / jnp.where(good, b, 1.0), other)


def first_kernel(core_ref, down_ref, up_ref, mine_ref, theirs_ref, high_ref, low_ref):
    @pl.when(pl.program_id(0) == 0)
    def _():
        lower, upper = halves(up_ref[0], up_ref[1])
        swap = core_ref[0] == 1
        for k, half in enumerate((jnp.where(swap, upper, lower), jnp.where(swap, lower, upper))):
            cols = slice(128 * k, 128 * k + 128)
            for rows, field in ((slice(0, OWN), half), (slice(OWN, 2 * OWN), -turn(half))):
                high, low = split(field)
                high_ref[rows, cols] = high
                low_ref[rows, cols] = low

    total = None
    for k in range(2):
        high, low = split(down_ref[k])
        rows = slice(OWN * k, OWN * (k + 1))
        part = dot(high, high_ref[rows]) + dot(high, low_ref[rows]) + dot(low, high_ref[rows])
        total = part if total is None else total + part
    mine_ref[...] = total[:, :128]
    theirs_ref[...] = total[:, 128:]


def first_adjoint(core, downgoing, upgoing):
    step = 512
    out = jax.ShapeDtypeStruct((ROWS, 128), F32)
    out_spec = pl.BlockSpec((step, 128), lambda i: (i, 0))
    return pl.pallas_call(
        first_kernel,
        grid=(ROWS // step,),
        in_specs=[
            SMEM,
            pl.BlockSpec((2, step, OWN), lambda i: (0, i, 0)),
            pl.BlockSpec((2, OWN, 128), lambda i: (0, 0, 0)),
        ],
        out_specs=(out_spec, out_spec),
        out_shape=(out, out),
        scratch_shapes=[pltpu.VMEM((2 * OWN, 256), BF16), pltpu.VMEM((2 * OWN, 256), BF16)],
        compiler_params=PARAMS,
        name="first_adjoint",
    )(core, downgoing, upgoing)


def forward_step(piece, own_ref, other_ref, image_ref, keep):
    total = None
    for k, field in enumerate((piece, turn(piece))):
        high, low = split(field.T)
        both = jnp.concatenate([high, low], axis=0)
        blocks = []
        for j, ref in enumerate((own_ref, other_ref)):
            down_high, down_low = split(ref[k])
            keep(k, j, down_high, down_low)
            wide = dot(both, down_high)
            blocks.append(wide[:128] + wide[128:] + dot(high, down_low))
        part = jnp.concatenate(blocks, axis=1)
        total = part if total is None else total + part
    return total


def normal_kernel(g_ref, own_ref, other_ref, q_ref, image_out_ref, high_ref, low_ref, image_ref, w_ref):
    i = pl.program_id(0)

    @pl.when(i < STEPS)
    def _():
        rows = pl.ds(pl.multiple_of(i * STEP, STEP), STEP)

        def keep(k, j, high, low):
            cols = slice(2 * OWN * k + OWN * j, 2 * OWN * k + OWN * (j + 1))
            high_ref[rows, cols] = high
            low_ref[rows, cols] = low

        part = forward_step(g_ref[rows], own_ref, other_ref, image_ref, keep)

        @pl.when(i == 0)
        def _():
            image_ref[...] = part

        @pl.when(i > 0)
        def _():
            image_ref[...] += part

    @pl.when(i == STEPS)
    def _():
        image = image_ref[...].T
        image_out_ref[...] = image
        for rows, field in ((slice(0, 512), image), (slice(512, 1024), -turn(image))):
            high, low = split(field)
            w_ref[rows, :128] = high
            w_ref[rows, 128:] = low

    @pl.when(i >= STEPS)
    def _():
        rows = pl.ds(pl.multiple_of((i - STEPS) * STEP, STEP), STEP)
        wide = dot(high_ref[rows], w_ref[...])
        q_ref[...] = wide[:, :128] + wide[:, 128:] + dot(low_ref[rows], w_ref[:, :128])


def normal(g, own, other):
    down = pl.BlockSpec((2, STEP, OWN), lambda i: (0, jnp.minimum(i, STEPS - 1), 0))
    return pl.pallas_call(
        normal_kernel,
        grid=(2 * STEPS,),
        in_specs=[pl.BlockSpec((ROWS, 128), lambda i: (0, 0)), down, down],
        out_specs=(
            pl.BlockSpec((STEP, 128), lambda i: (jnp.maximum(i - STEPS, 0), 0)),
            pl.BlockSpec((2 * OWN, 128), lambda i: (0, 0)),
        ),
        out_shape=(jax.ShapeDtypeStruct((ROWS, 128), F32), jax.ShapeDtypeStruct((2 * OWN, 128), F32)),
        scratch_shapes=[
            pltpu.VMEM((ROWS, 4 * OWN), BF16),
            pltpu.VMEM((ROWS, 4 * OWN), BF16),
            pltpu.VMEM((128, 2 * OWN), F32),
            pltpu.VMEM((4 * OWN, 256), BF16),
        ],
        compiler_params=PARAMS,
        name="normal_product",
    )(g, own, other)


def second_kernel(place_ref, g_ref, q_ref, own_ref, other_ref, image0_ref, keep_ref, give_ref, row_ref, p_ref, image_ref, scalar_ref):
    i = pl.program_id(0)

    @pl.when(i == 0)
    def _():
        g, q = g_ref[...], q_ref[...]
        gamma0 = jnp.sum(g * g)
        m = jnp.sum(g * q)
        g1 = g - ratio(gamma0, m, 1.0) * q
        gamma1 = jnp.sum(g1 * g1)
        p_ref[...] = g1 + ratio(gamma1, gamma0, 0.0) * g
        scalar_ref[0] = gamma0
        scalar_ref[1] = m
        scalar_ref[2] = gamma1

    rows = pl.ds(pl.multiple_of(i * STEP, STEP), STEP)
    part = forward_step(p_ref[rows], own_ref, other_ref, image_ref, lambda *_: None)

    @pl.when(i == 0)
    def _():
        image_ref[...] = part

    @pl.when(i > 0)
    def _():
        image_ref[...] += part

    @pl.when(i == STEPS - 1)
    def _():
        image = image_ref[...].T
        square = jnp.sum(image * image)
        lane = lax.broadcasted_iota(jnp.int32, row_ref.shape, 2)
        row_ref[...] = jnp.where(
            lane == 0,
            square,
            jnp.where(lane == 1, scalar_ref[0], jnp.where(lane == 2, scalar_ref[1], scalar_ref[2])),
        )
        core, chip = place_ref[0], place_ref[1]
        own_rows = pl.ds(pl.multiple_of(chip * 64 + core * 32, 32), 32)
        other_rows = pl.ds(pl.multiple_of(chip * 64 + (1 - core) * 32, 32), 32)
        keep_ref[:OWN] = image0_ref[:OWN]
        keep_ref[OWN : 2 * OWN] = image[:OWN]
        keep_ref[2 * OWN : 2 * OWN + 32] = g_ref[own_rows]
        keep_ref[2 * OWN + 32 :] = p_ref[own_rows]
        give_ref[:OWN] = image0_ref[OWN:]
        give_ref[OWN : 2 * OWN] = image[OWN:]
        give_ref[2 * OWN : 2 * OWN + 32] = g_ref[other_rows]
        give_ref[2 * OWN + 32 :] = p_ref[other_rows]


def second_forward(place, g, q, own, other, image0):
    down = pl.BlockSpec((2, STEP, OWN), lambda i: (0, i, 0))
    whole = lambda *shape: pl.BlockSpec(shape, lambda i: (0,) * len(shape))
    pack = jax.ShapeDtypeStruct((2 * OWN + 64, 128), F32)
    return pl.pallas_call(
        second_kernel,
        grid=(STEPS,),
        in_specs=[SMEM, whole(ROWS, 128), whole(ROWS, 128), down, down, whole(2 * OWN, 128)],
        out_specs=(whole(*pack.shape), whole(*pack.shape), whole(2 * CHIPS, 8, 128)),
        out_shape=(pack, pack, jax.ShapeDtypeStruct((2 * CHIPS, 8, 128), F32)),
        scratch_shapes=[
            pltpu.VMEM((ROWS, 128), F32),
            pltpu.VMEM((128, 2 * OWN), F32),
            pltpu.SMEM((4,), F32),
        ],
        compiler_params=PARAMS,
        name="second_forward",
    )(place, g, q, own, other, image0)


def last_kernel(place_ref, got_ref, up_ref, keep_ref, take_ref, filt_ref, residual_ref):
    got = got_ref[:, 0, :]
    odd = lax.broadcasted_iota(jnp.int32, got.shape, 0) % 2 == 1
    squares = jnp.sum(jnp.where(odd, 0.0, got), axis=0, keepdims=True), jnp.sum(jnp.where(odd, got, 0.0), axis=0, keepdims=True)
    coefficient = [(squares[c][:, 0:1], got[c : c + 1, 1:2], got[c : c + 1, 2:3], got[c : c + 1, 3:4]) for c in range(2)]
    gamma = coefficient[0][1] + coefficient[1][1]
    alpha0 = gamma / (coefficient[0][2] + coefficient[1][2])
    gamma_new = 0.0
    scales = []
    for square, gamma0, m, gamma1 in coefficient:
        s = alpha0 / ratio(gamma0, m, 1.0)
        scales.append(s)
        gamma_new = gamma_new + s * s * gamma1 + (1.0 - s) * (1.0 - s) * gamma0
    beta = gamma_new / gamma
    norm = 0.0
    shifts = []
    for s, (square, gamma0, m, gamma1) in zip(scales, coefficient):
        e = beta + 1.0 - s - s * ratio(gamma1, gamma0, 0.0)
        shifts.append(e)
        norm = norm + s * s * square + e * e * m
    alpha1 = gamma_new / norm
    for_g = [alpha0 + alpha1 * e for e in shifts]
    for_p = [alpha1 * s for s in scales]

    low = place_ref[0] == 0

    def both(rows):
        mine, theirs = keep_ref[rows], take_ref[rows]
        return jnp.where(low, mine, theirs), jnp.where(low, theirs, mine)

    def combine(first, second):
        columns = [for_g[c] * first[c] + for_p[c] * second[c] for c in range(2)]
        return halves(*columns)

    re, im = combine(both(slice(0, OWN)), both(slice(OWN, 2 * OWN)))
    residual_ref[0] = up_ref[0] - re
    residual_ref[1] = up_ref[1] - im
    re, im = combine(both(slice(2 * OWN, 2 * OWN + 32)), both(slice(2 * OWN + 32, 2 * OWN + 64)))
    filt_ref[:, 0, :] = re
    filt_ref[:, 1, :] = im


def last(place, got, upgoing, keep, take):
    return pl.pallas_call(
        last_kernel,
        in_specs=[SMEM, VMEM, VMEM, VMEM, VMEM],
        out_specs=(VMEM, VMEM),
        out_shape=(jax.ShapeDtypeStruct((32, 2, 128), F32), jax.ShapeDtypeStruct((2, OWN, 128), F32)),
        compiler_params=PARAMS,
        name="last_update",
    )(place, got, upgoing, keep, take)


def exchange(blocks):
    return lax.all_to_all(blocks, ("y", "x"), 0, 0, tiled=True)


def all_sum(partial):
    parts = exchange(partial.reshape(CHIPS, ROWS // CHIPS, 128))
    block = jnp.sum(parts, axis=0)
    return exchange(jnp.broadcast_to(block, parts.shape)).reshape(ROWS, 128)


def on_device(downgoing, upgoing):
    core = lax.axis_index("core").astype(jnp.int32)
    chip = (lax.axis_index("y") * 4 + lax.axis_index("x")).astype(jnp.int32)
    place = jnp.stack([core, chip])
    mine, theirs = first_adjoint(place, downgoing, upgoing)
    theirs = lax.ppermute(theirs, SRC, SWAP)
    other_down, theirs = lax.optimization_barrier((downgoing, theirs))
    other_down = lax.ppermute(other_down, SRC, SWAP)
    g = all_sum(mine + theirs)
    q, image0 = normal(g, downgoing, other_down)
    q = all_sum(q)
    keep, give, row = second_forward(place, g, q, downgoing, other_down, image0)
    take = lax.ppermute(give, SRC, SWAP)
    got = lax.all_to_all(row, SRC, 0, 0, tiled=True)
    return last(place, got, upgoing, keep, take)


def solution(mesh):
    devices = mesh.devices.reshape(mesh.shape["freq"], 8, 4, 2)
    return jax.shard_map(
        on_device,
        mesh=Mesh(devices, ("freq",) + SRC),
        in_specs=(P("freq", None, SRC), P("freq", SRC, None)),
        out_specs=(P(SRC, "freq", None), P("freq", SRC, None)),
        check_vma=False,
    )
```

```python
import jax
import jax.numpy as jnp
from jax import lax
from jax.experimental import pallas as pl
from jax.experimental.pallas import tpu as pltpu
from jax.sharding import Mesh, PartitionSpec as P

SRC = ("y", "x", "core")
CHIPS = 32
ROWS = 2048
OWN = 256
STEP = 512
STEPS = ROWS // STEP
SWAP = [(i, i ^ 1) for i in range(2 * CHIPS)]
VMEM = pl.BlockSpec(memory_space=pltpu.VMEM)
F32 = jnp.float32
BF16 = jnp.bfloat16


def dot(a, b):
    return jnp.dot(a, b, preferred_element_type=F32)


def split(x):
    high = x.astype(BF16)
    return high, (x - high.astype(F32)).astype(BF16)


def lanes(x):
    return lax.broadcasted_iota(jnp.int32, x.shape, x.ndim - 1) < 64


def turn(z):
    swapped = pltpu.roll(z, 64, 1)
    return jnp.where(lanes(z), -swapped, swapped)


def halves(re, im):
    first = lanes(re)
    return jnp.where(first, re, pltpu.roll(im, 64, 1)), jnp.where(first, pltpu.roll(re, 64, 1), im)


def ratio(a, b, other):
    good = b > 0
    return jnp.where(good, a / jnp.where(good, b, 1.0), other)


def whole_rows(ref, i):
    blocks = [ref[:, y].reshape(STEP // 2, 128) for y in (2 * i, 2 * i + 1)]
    return jnp.concatenate(blocks, axis=0)


def put_rows(ref, i, value):
    for k in range(2):
        ref[:, 2 * i + k] = value[k * STEP // 2 : (k + 1) * STEP // 2].reshape(4, 64, 128)


def first_kernel(down_hbm, up_ref, mine_ref, theirs_ref, down_ref, high_ref, low_ref, sem):
    copies = []
    for i in range(STEPS):
        rows = pl.ds(i * STEP, STEP)
        copies.append(pltpu.make_async_copy(down_hbm.at[:, rows], down_ref.at[:, rows], sem.at[i]))
        copies[-1].start()
    lower, upper = halves(up_ref[0], up_ref[1])
    swap = lax.axis_index("core") == 1
    for k, half in enumerate((jnp.where(swap, upper, lower), jnp.where(swap, lower, upper))):
        cols = slice(128 * k, 128 * k + 128)
        for rows, field in ((slice(0, OWN), half), (slice(OWN, 2 * OWN), -turn(half))):
            high_ref[rows, cols], low_ref[rows, cols] = split(field)
    for i in range(STEPS):
        copies[i].wait()
        total = None
        for k in range(2):
            high, low = split(down_ref[k, i * STEP : (i + 1) * STEP])
            rows = slice(OWN * k, OWN * (k + 1))
            part = dot(high, high_ref[rows]) + dot(high, low_ref[rows]) + dot(low, high_ref[rows])
            total = part if total is None else total + part
        put_rows(mine_ref, i, total[:, :128])
        put_rows(theirs_ref, i, total[:, 128:])


def first_adjoint(downgoing, upgoing):
    out = jax.ShapeDtypeStruct((4, 8, 64, 128), F32)
    return pl.pallas_call(
        first_kernel,
        in_specs=[pl.BlockSpec(memory_space=pl.ANY), VMEM],
        out_specs=(VMEM, VMEM, VMEM),
        out_shape=(out, out, jax.ShapeDtypeStruct(downgoing.shape, F32)),
        scratch_shapes=[
            pltpu.VMEM((2 * OWN, 256), BF16),
            pltpu.VMEM((2 * OWN, 256), BF16),
            pltpu.SemaphoreType.DMA((STEPS,)),
        ],
        compiler_params=pltpu.CompilerParams(vmem_limit_bytes=16 * 2**20),
        name="first_adjoint",
    )(downgoing, upgoing)


def forward_step(piece, own_ref, other_ref, rows, keep):
    total = None
    for k, field in enumerate((piece, turn(piece))):
        high, low = split(field.T)
        both = jnp.concatenate([high, low], axis=0)
        blocks = []
        for j, ref in enumerate((own_ref, other_ref)):
            down_high, down_low = split(ref[k, rows])
            keep(slice(2 * OWN * k + OWN * j, 2 * OWN * k + OWN * (j + 1)), down_high, down_low)
            wide = dot(both, down_high)
            blocks.append(wide[:128] + wide[128:] + dot(high, down_low))
        part = jnp.concatenate(blocks, axis=1)
        total = part if total is None else total + part
    return total


def normal_kernel(g_ref, own_ref, other_ref, q_ref, image_ref, high_ref, low_ref, w_ref):
    total = None
    for i in range(STEPS):
        rows = slice(i * STEP, (i + 1) * STEP)

        def keep(cols, high, low):
            high_ref[rows, cols] = high
            low_ref[rows, cols] = low

        part = forward_step(whole_rows(g_ref, i), own_ref, other_ref, rows, keep)
        total = part if total is None else total + part
    image = total.T
    image_ref[...] = image
    for rows, field in ((slice(0, 512), image), (slice(512, 1024), -turn(image))):
        w_ref[rows, :128], w_ref[rows, 128:] = split(field)
    for i in range(STEPS):
        rows = slice(i * STEP, (i + 1) * STEP)
        wide = dot(high_ref[rows], w_ref[...])
        put_rows(q_ref, i, wide[:, :128] + wide[:, 128:] + dot(low_ref[rows], w_ref[:, :128]))


def normal(g, own, other):
    return pl.pallas_call(
        normal_kernel,
        in_specs=[VMEM, VMEM, VMEM],
        out_specs=(VMEM, VMEM),
        out_shape=(jax.ShapeDtypeStruct(g.shape, F32), jax.ShapeDtypeStruct((2 * OWN, 128), F32)),
        scratch_shapes=[
            pltpu.VMEM((ROWS, 4 * OWN), BF16),
            pltpu.VMEM((ROWS, 4 * OWN), BF16),
            pltpu.VMEM((4 * OWN, 256), BF16),
        ],
        compiler_params=pltpu.CompilerParams(vmem_limit_bytes=40 * 2**20),
        name="normal_product",
    )(g, own, other)


def second_kernel(g_ref, q_ref, own_ref, other_ref, image0_ref, keep_ref, give_ref, row_ref, p_ref):
    g, q = g_ref[...], q_ref[...]
    gamma0 = jnp.sum(g * g)
    m = jnp.sum(g * q)
    g1 = g - ratio(gamma0, m, 1.0) * q
    gamma1 = jnp.sum(g1 * g1)
    p_ref[...] = g1 + ratio(gamma1, gamma0, 0.0) * g

    total = None
    for i in range(STEPS):
        rows = slice(i * STEP, (i + 1) * STEP)
        part = forward_step(whole_rows(p_ref, i), own_ref, other_ref, rows, lambda *_: None)
        total = part if total is None else total + part
    image = total.T
    square = jnp.sum(image * image)
    lane = lax.broadcasted_iota(jnp.int32, row_ref.shape, 2)
    row_ref[...] = jnp.where(
        lane == 0, square, jnp.where(lane == 1, gamma0, jnp.where(lane == 2, m, gamma1))
    )
    x, y, core = lax.axis_index("x"), lax.axis_index("y"), lax.axis_index("core")
    own_rows = pl.ds(pl.multiple_of(core * 32, 32), 32)
    other_rows = pl.ds(pl.multiple_of((1 - core) * 32, 32), 32)
    for ref, sources, receivers in ((keep_ref, slice(0, OWN), own_rows), (give_ref, slice(OWN, 2 * OWN), other_rows)):
        ref[:OWN] = image0_ref[sources]
        ref[OWN : 2 * OWN] = image[sources]
        ref[2 * OWN : 2 * OWN + 32] = g_ref[x, y, receivers]
        ref[2 * OWN + 32 :] = p_ref[x, y, receivers]


def second_forward(g, q, own, other, image0):
    pack = jax.ShapeDtypeStruct((2 * OWN + 64, 128), F32)
    return pl.pallas_call(
        second_kernel,
        in_specs=[VMEM] * 5,
        out_specs=(VMEM,) * 3,
        out_shape=(pack, pack, jax.ShapeDtypeStruct((2 * CHIPS, 1, 128), F32)),
        scratch_shapes=[pltpu.VMEM(g.shape, F32)],
        compiler_params=pltpu.CompilerParams(vmem_limit_bytes=40 * 2**20),
        name="second_forward",
    )(g, q, own, other, image0)


def last_kernel(got_ref, up_ref, keep_ref, take_ref, filt_ref, residual_ref):
    got = got_ref[:, 0, :]
    odd = lax.broadcasted_iota(jnp.int32, got.shape, 0) % 2 == 1
    squares = jnp.sum(jnp.where(odd, 0.0, got), axis=0, keepdims=True), jnp.sum(jnp.where(odd, got, 0.0), axis=0, keepdims=True)
    coefficient = [(squares[c][:, 0:1], got[c : c + 1, 1:2], got[c : c + 1, 2:3], got[c : c + 1, 3:4]) for c in range(2)]
    gamma = coefficient[0][1] + coefficient[1][1]
    alpha0 = gamma / (coefficient[0][2] + coefficient[1][2])
    gamma_new = 0.0
    scales = []
    for square, gamma0, m, gamma1 in coefficient:
        s = alpha0 / ratio(gamma0, m, 1.0)
        scales.append(s)
        gamma_new = gamma_new + s * s * gamma1 + (1.0 - s) * (1.0 - s) * gamma0
    beta = gamma_new / gamma
    norm = 0.0
    shifts = []
    for s, (square, gamma0, m, gamma1) in zip(scales, coefficient):
        e = beta + 1.0 - s - s * ratio(gamma1, gamma0, 0.0)
        shifts.append(e)
        norm = norm + s * s * square + e * e * m
    alpha1 = gamma_new / norm
    for_g = [alpha0 + alpha1 * e for e in shifts]
    for_p = [alpha1 * s for s in scales]

    low = lax.axis_index("core") == 0

    def both(rows):
        mine, theirs = keep_ref[rows], take_ref[rows]
        return jnp.where(low, mine, theirs), jnp.where(low, theirs, mine)

    def combine(first, second):
        columns = [for_g[c] * first[c] + for_p[c] * second[c] for c in range(2)]
        return halves(*columns)

    re, im = combine(both(slice(0, OWN)), both(slice(OWN, 2 * OWN)))
    residual_ref[0] = up_ref[0] - re
    residual_ref[1] = up_ref[1] - im
    re, im = combine(both(slice(2 * OWN, 2 * OWN + 32)), both(slice(2 * OWN + 32, 2 * OWN + 64)))
    filt_ref[:, 0, :] = re
    filt_ref[:, 1, :] = im


def last(got, upgoing, keep, take):
    return pl.pallas_call(
        last_kernel,
        in_specs=[VMEM] * 4,
        out_specs=(VMEM, VMEM),
        out_shape=(jax.ShapeDtypeStruct((32, 2, 128), F32), jax.ShapeDtypeStruct((2, OWN, 128), F32)),
        compiler_params=pltpu.CompilerParams(vmem_limit_bytes=8 * 2**20),
        name="last_update",
    )(got, upgoing, keep, take)


def exchange(blocks, axis):
    return lax.all_to_all(blocks, axis, 0, 0, tiled=True)


def all_sum(partial):
    row = jnp.sum(exchange(partial, "x"), axis=0)
    block = jnp.sum(exchange(row, "y"), axis=0)
    row = exchange(jnp.broadcast_to(block, row.shape), "y")
    return exchange(jnp.broadcast_to(row, partial.shape), "x")


def on_device(downgoing, upgoing):
    mine, theirs, down = first_adjoint(downgoing, upgoing)
    theirs = lax.ppermute(theirs, SRC, SWAP)
    down, theirs = lax.optimization_barrier((down, theirs))
    other_down = lax.ppermute(down, SRC, SWAP)
    g = all_sum(mine + theirs)
    q, image0 = normal(g, down, other_down)
    q = all_sum(q)
    keep, give, row = second_forward(g, q, down, other_down, image0)
    take = lax.ppermute(give, SRC, SWAP)
    got = lax.all_to_all(row, SRC, 0, 0, tiled=True)
    return last(got, upgoing, keep, take)


def solution(mesh):
    devices = mesh.devices.reshape(mesh.shape["freq"], 8, 4, 2)
    return jax.shard_map(
        on_device,
        mesh=Mesh(devices, ("freq",) + SRC),
        in_specs=(P("freq", None, SRC), P("freq", SRC, None)),
        out_specs=(P(SRC, "freq", None), P("freq", SRC, None)),
        check_vma=False,
    )
```

```python
import jax
import jax.numpy as jnp
from jax import lax
from jax.experimental import pallas as pl
from jax.experimental.pallas import tpu as pltpu
from jax.sharding import Mesh, PartitionSpec as P

SRC = ("y", "x", "core")
CHIPS = 32
ROWS = 2048
OWN = 256
STEP = 512
STEPS = ROWS // STEP
SWAP = [(i, i ^ 1) for i in range(2 * CHIPS)]
VMEM = pl.BlockSpec(memory_space=pltpu.VMEM)
HBM = pl.BlockSpec(memory_space=pltpu.HBM)
F32 = jnp.float32
BF16 = jnp.bfloat16


def in_vmem(*arrays):
    return [pltpu.with_memory_space_constraint(a, pltpu.VMEM) for a in arrays]


def in_hbm(*arrays):
    return [pltpu.with_memory_space_constraint(a, pltpu.HBM) for a in arrays]


def dot(a, b):
    return jnp.dot(a, b, preferred_element_type=F32)


def split(x):
    high = x.astype(BF16)
    return high, (x - high.astype(F32)).astype(BF16)


def lanes(x):
    return lax.broadcasted_iota(jnp.int32, x.shape, x.ndim - 1) < 64


def turn(z):
    swapped = pltpu.roll(z, 64, 1)
    return jnp.where(lanes(z), -swapped, swapped)


def halves(re, im):
    first = lanes(re)
    return jnp.where(first, re, pltpu.roll(im, 64, 1)), jnp.where(first, pltpu.roll(re, 64, 1), im)


def ratio(a, b, other):
    good = b > 0
    return jnp.where(good, a / jnp.where(good, b, 1.0), other)


def whole_rows(ref, i):
    blocks = [ref[:, y].reshape(STEP // 2, 128) for y in (2 * i, 2 * i + 1)]
    return jnp.concatenate(blocks, axis=0)


def put_rows(ref, i, value):
    for k in range(2):
        ref[:, 2 * i + k] = value[k * STEP // 2 : (k + 1) * STEP // 2].reshape(4, 64, 128)


def first_kernel(down_hbm, up_hbm, mine_ref, theirs_ref, down_ref, up_ref, high_ref, low_ref, sem):
    field_copy = pltpu.make_async_copy(up_hbm, up_ref, sem.at[0])
    field_copy.start()
    down_copy = pltpu.make_async_copy(down_hbm, down_ref, sem.at[1])
    down_copy.start()
    field_copy.wait()
    lower, upper = halves(up_ref[0], up_ref[1])
    swap = lax.axis_index("core") == 1
    for k, half in enumerate((jnp.where(swap, upper, lower), jnp.where(swap, lower, upper))):
        cols = slice(128 * k, 128 * k + 128)
        for rows, field in ((slice(0, OWN), half), (slice(OWN, 2 * OWN), -turn(half))):
            high_ref[rows, cols], low_ref[rows, cols] = split(field)
    down_copy.wait()
    parts = [split(down_ref[k]) for k in range(2)]
    high = jnp.concatenate([parts[0][0], parts[1][0]], axis=1)
    low = jnp.concatenate([parts[0][1], parts[1][1]], axis=1)
    total = dot(high, high_ref[...]) + dot(high, low_ref[...]) + dot(low, high_ref[...])
    for i in range(STEPS):
        rows = slice(i * STEP, (i + 1) * STEP)
        put_rows(mine_ref, i, total[rows, :128])
        put_rows(theirs_ref, i, total[rows, 128:])


def first_adjoint(downgoing, upgoing):
    out = pltpu.VMEM((4, 8, 64, 128), F32)
    return pl.pallas_call(
        first_kernel,
        in_specs=[HBM, HBM],
        out_specs=(VMEM, VMEM, VMEM),
        out_shape=(out, out, pltpu.VMEM(downgoing.shape, F32)),
        scratch_shapes=[
            pltpu.VMEM(upgoing.shape, F32),
            pltpu.VMEM((2 * OWN, 256), BF16),
            pltpu.VMEM((2 * OWN, 256), BF16),
            pltpu.SemaphoreType.DMA((2,)),
        ],
        compiler_params=pltpu.CompilerParams(vmem_limit_bytes=24 * 2**20),
        name="first_adjoint",
    )(*in_hbm(downgoing, upgoing))


def forward_step(piece, own_ref, other_ref, rows, keep):
    total = None
    for k, field in enumerate((piece, turn(piece))):
        high, low = split(field.T)
        both = jnp.concatenate([high, low], axis=0)
        blocks = []
        for j, ref in enumerate((own_ref, other_ref)):
            down_high, down_low = split(ref[k, rows])
            keep(slice(2 * OWN * k + OWN * j, 2 * OWN * k + OWN * (j + 1)), down_high, down_low)
            wide = dot(both, down_high)
            blocks.append(wide[:128] + wide[128:] + dot(high, down_low))
        part = jnp.concatenate(blocks, axis=1)
        total = part if total is None else total + part
    return total


def normal_kernel(g_ref, own_ref, other_ref, q_ref, image_ref, high_ref, low_ref, w_ref):
    total = None
    for i in range(STEPS):
        rows = slice(i * STEP, (i + 1) * STEP)

        def keep(cols, high, low):
            high_ref[rows, cols] = high
            low_ref[rows, cols] = low

        part = forward_step(whole_rows(g_ref, i), own_ref, other_ref, rows, keep)
        total = part if total is None else total + part
    image = total.T
    image_ref[...] = image
    for rows, field in ((slice(0, 512), image), (slice(512, 1024), -turn(image))):
        w_ref[rows, :128], w_ref[rows, 128:] = split(field)
    for i in range(STEPS):
        rows = slice(i * STEP, (i + 1) * STEP)
        wide = dot(high_ref[rows], w_ref[...])
        put_rows(q_ref, i, wide[:, :128] + wide[:, 128:] + dot(low_ref[rows], w_ref[:, :128]))


def normal(g, own, other):
    return pl.pallas_call(
        normal_kernel,
        in_specs=[VMEM, VMEM, VMEM],
        out_specs=(VMEM, VMEM),
        out_shape=(pltpu.VMEM(g.shape, F32), pltpu.VMEM((2 * OWN, 128), F32)),
        scratch_shapes=[
            pltpu.VMEM((ROWS, 4 * OWN), BF16),
            pltpu.VMEM((ROWS, 4 * OWN), BF16),
            pltpu.VMEM((4 * OWN, 256), BF16),
        ],
        compiler_params=pltpu.CompilerParams(vmem_limit_bytes=28 * 2**20),
        name="normal_product",
    )(*in_vmem(g, own, other))


def second_kernel(g_ref, q_ref, own_ref, other_ref, image0_ref, keep_ref, give_ref, row_ref, p_ref):
    g, q = g_ref[...], q_ref[...]
    gamma0 = jnp.sum(g * g)
    m = jnp.sum(g * q)
    g1 = g - ratio(gamma0, m, 1.0) * q
    gamma1 = jnp.sum(g1 * g1)
    p_ref[...] = g1 + ratio(gamma1, gamma0, 0.0) * g

    total = None
    for i in range(STEPS):
        rows = slice(i * STEP, (i + 1) * STEP)
        part = forward_step(whole_rows(p_ref, i), own_ref, other_ref, rows, lambda *_: None)
        total = part if total is None else total + part
    image = total.T
    square = jnp.sum(image * image)
    lane = lax.broadcasted_iota(jnp.int32, row_ref.shape, 2)
    row_ref[...] = jnp.where(
        lane == 0, square, jnp.where(lane == 1, gamma0, jnp.where(lane == 2, m, gamma1))
    )
    x, y, core = lax.axis_index("x"), lax.axis_index("y"), lax.axis_index("core")
    own_rows = pl.ds(pl.multiple_of(core * 32, 32), 32)
    other_rows = pl.ds(pl.multiple_of((1 - core) * 32, 32), 32)
    for ref, sources, receivers in ((keep_ref, slice(0, OWN), own_rows), (give_ref, slice(OWN, 2 * OWN), other_rows)):
        ref[:OWN] = image0_ref[sources]
        ref[OWN : 2 * OWN] = image[sources]
        ref[2 * OWN : 2 * OWN + 32] = g_ref[x, y, receivers]
        ref[2 * OWN + 32 :] = p_ref[x, y, receivers]


def second_forward(g, q, own, other, image0):
    pack = pltpu.VMEM((2 * OWN + 64, 128), F32)
    return pl.pallas_call(
        second_kernel,
        in_specs=[VMEM] * 5,
        out_specs=(VMEM,) * 3,
        out_shape=(pack, pack, pltpu.VMEM((2 * CHIPS, 1, 128), F32)),
        scratch_shapes=[pltpu.VMEM(g.shape, F32)],
        compiler_params=pltpu.CompilerParams(vmem_limit_bytes=16 * 2**20),
        name="second_forward",
    )(*in_vmem(g, q, own, other, image0))


def last_kernel(got_ref, up_ref, keep_ref, take_ref, filt_ref, residual_ref):
    got = got_ref[:, 0, :]
    odd = lax.broadcasted_iota(jnp.int32, got.shape, 0) % 2 == 1
    squares = jnp.sum(jnp.where(odd, 0.0, got), axis=0, keepdims=True), jnp.sum(jnp.where(odd, got, 0.0), axis=0, keepdims=True)
    coefficient = [(squares[c][:, 0:1], got[c : c + 1, 1:2], got[c : c + 1, 2:3], got[c : c + 1, 3:4]) for c in range(2)]
    gamma = coefficient[0][1] + coefficient[1][1]
    alpha0 = gamma / (coefficient[0][2] + coefficient[1][2])
    gamma_new = 0.0
    scales = []
    for square, gamma0, m, gamma1 in coefficient:
        s = alpha0 / ratio(gamma0, m, 1.0)
        scales.append(s)
        gamma_new = gamma_new + s * s * gamma1 + (1.0 - s) * (1.0 - s) * gamma0
    beta = gamma_new / gamma
    norm = 0.0
    shifts = []
    for s, (square, gamma0, m, gamma1) in zip(scales, coefficient):
        e = beta + 1.0 - s - s * ratio(gamma1, gamma0, 0.0)
        shifts.append(e)
        norm = norm + s * s * square + e * e * m
    alpha1 = gamma_new / norm
    for_g = [alpha0 + alpha1 * e for e in shifts]
    for_p = [alpha1 * s for s in scales]

    low = lax.axis_index("core") == 0

    def both(rows):
        mine, theirs = keep_ref[rows], take_ref[rows]
        return jnp.where(low, mine, theirs), jnp.where(low, theirs, mine)

    def combine(first, second):
        columns = [for_g[c] * first[c] + for_p[c] * second[c] for c in range(2)]
        return halves(*columns)

    re, im = combine(both(slice(0, OWN)), both(slice(OWN, 2 * OWN)))
    residual_ref[0] = up_ref[0] - re
    residual_ref[1] = up_ref[1] - im
    re, im = combine(both(slice(2 * OWN, 2 * OWN + 32)), both(slice(2 * OWN + 32, 2 * OWN + 64)))
    filt_ref[:, 0, :] = re
    filt_ref[:, 1, :] = im


def last(got, upgoing, keep, take):
    return pl.pallas_call(
        last_kernel,
        in_specs=[VMEM] * 4,
        out_specs=(VMEM, VMEM),
        out_shape=(jax.ShapeDtypeStruct((32, 2, 128), F32), jax.ShapeDtypeStruct((2, OWN, 128), F32)),
        compiler_params=pltpu.CompilerParams(vmem_limit_bytes=12 * 2**20),
        name="last_update",
    )(got, upgoing, keep, take)


def small(body, shape, name, *arrays):
    return pl.pallas_call(
        body,
        in_specs=[VMEM] * len(arrays),
        out_specs=VMEM,
        out_shape=pltpu.VMEM(shape, F32),
        compiler_params=pltpu.CompilerParams(vmem_limit_bytes=4 * 2**20),
        name=name,
    )(*in_vmem(*arrays))


def add_kernel(a_ref, b_ref, out_ref):
    out_ref[...] = a_ref[...] + b_ref[...]


def total(ref):
    value = ref[0]
    for k in range(1, ref.shape[0]):
        value = value + ref[k]
    return value


def sum_kernel(ref, out_ref):
    out_ref[...] = total(ref)


def sum_repeat_kernel(ref, out_ref):
    value = total(ref)
    for k in range(out_ref.shape[0]):
        out_ref[k] = value


def repeat_kernel(ref, out_ref):
    value = ref[...]
    for k in range(out_ref.shape[0]):
        out_ref[k] = value


def exchange(blocks, axis):
    return lax.all_to_all(blocks, axis, 0, 0, tiled=True)


def all_sum(partial):
    row = small(sum_kernel, partial.shape[1:], "sum_x", exchange(partial, "x"))
    row = small(sum_repeat_kernel, row.shape, "sum_y", exchange(row, "y"))
    whole = small(repeat_kernel, partial.shape, "repeat_x", exchange(row, "y"))
    return exchange(whole, "x")


def on_device(downgoing, upgoing):
    mine, theirs, down = first_adjoint(downgoing, upgoing)
    theirs = lax.ppermute(theirs, SRC, SWAP)
    down, theirs = lax.optimization_barrier((down, theirs))
    other_down = lax.ppermute(down, SRC, SWAP)
    g = all_sum(small(add_kernel, mine.shape, "add_cores", mine, theirs))
    q, image0 = normal(g, down, other_down)
    q = all_sum(q)
    keep, give, row = second_forward(g, q, down, other_down, image0)
    take = lax.ppermute(give, SRC, SWAP)
    got = lax.all_to_all(row, SRC, 0, 0, tiled=True)
    return last(got, upgoing, keep, take)


def solution(mesh):
    devices = mesh.devices.reshape(mesh.shape["freq"], 8, 4, 2)
    return jax.shard_map(
        on_device,
        mesh=Mesh(devices, ("freq",) + SRC),
        in_specs=(P("freq", None, SRC), P("freq", SRC, None)),
        out_specs=(P(SRC, "freq", None), P("freq", SRC, None)),
        check_vma=False,
    )
```

```python
import jax
import jax.numpy as jnp
from jax import lax
from jax.experimental import pallas as pl
from jax.experimental.pallas import tpu as pltpu
from jax.sharding import Mesh, PartitionSpec as P

SRC = ("y_high", "y_low", "x", "core")
NEAR = ("y_low", "x")
CHIPS = 32
ROWS = 2048
OWN = 256
STEP = 512
STEPS = ROWS // STEP
SWAP = [(i, i ^ 1) for i in range(2 * CHIPS)]
VMEM = pl.BlockSpec(memory_space=pltpu.VMEM)
HBM = pl.BlockSpec(memory_space=pltpu.HBM)
F32 = jnp.float32
BF16 = jnp.bfloat16


def in_vmem(*arrays):
    return [pltpu.with_memory_space_constraint(a, pltpu.VMEM) for a in arrays]


def in_hbm(*arrays):
    return [pltpu.with_memory_space_constraint(a, pltpu.HBM) for a in arrays]


def dot(a, b):
    return jnp.dot(a, b, preferred_element_type=F32)


def split(x):
    high = x.astype(BF16)
    return high, (x - high.astype(F32)).astype(BF16)


def lanes(x):
    return lax.broadcasted_iota(jnp.int32, x.shape, x.ndim - 1) < 64


def turn(z):
    swapped = pltpu.roll(z, 64, 1)
    return jnp.where(lanes(z), -swapped, swapped)


def halves(re, im):
    first = lanes(re)
    return jnp.where(first, re, pltpu.roll(im, 64, 1)), jnp.where(first, pltpu.roll(re, 64, 1), im)


def ratio(a, b, other):
    good = b > 0
    return jnp.where(good, a / jnp.where(good, b, 1.0), other)


def whole_rows(ref, i):
    return ref[:, i].reshape(STEP, 128)


def put_rows(ref, i, value):
    ref[:, i] = value.reshape(8, 64, 128)


def first_kernel(down_hbm, up_hbm, mine_ref, theirs_ref, down_ref, up_ref, high_ref, low_ref, sem):
    field_copy = pltpu.make_async_copy(up_hbm, up_ref, sem.at[0])
    field_copy.start()
    down_copy = pltpu.make_async_copy(down_hbm, down_ref, sem.at[1])
    down_copy.start()
    field_copy.wait()
    lower, upper = halves(up_ref[0], up_ref[1])
    swap = lax.axis_index("core") == 1
    for k, half in enumerate((jnp.where(swap, upper, lower), jnp.where(swap, lower, upper))):
        cols = slice(128 * k, 128 * k + 128)
        for rows, field in ((slice(0, OWN), half), (slice(OWN, 2 * OWN), -turn(half))):
            high_ref[rows, cols], low_ref[rows, cols] = split(field)
    down_copy.wait()
    parts = [split(down_ref[k]) for k in range(2)]
    high = jnp.concatenate([parts[0][0], parts[1][0]], axis=1)
    low = jnp.concatenate([parts[0][1], parts[1][1]], axis=1)
    total = dot(high, high_ref[...]) + dot(high, low_ref[...]) + dot(low, high_ref[...])
    for i in range(STEPS):
        rows = slice(i * STEP, (i + 1) * STEP)
        put_rows(mine_ref, i, total[rows, :128])
        put_rows(theirs_ref, i, total[rows, 128:])


def first_adjoint(downgoing, upgoing):
    out = pltpu.VMEM((8, 4, 64, 128), F32)
    return pl.pallas_call(
        first_kernel,
        in_specs=[HBM, HBM],
        out_specs=(VMEM, VMEM, VMEM),
        out_shape=(out, out, pltpu.VMEM(downgoing.shape, F32)),
        scratch_shapes=[
            pltpu.VMEM(upgoing.shape, F32),
            pltpu.VMEM((2 * OWN, 256), BF16),
            pltpu.VMEM((2 * OWN, 256), BF16),
            pltpu.SemaphoreType.DMA((2,)),
        ],
        compiler_params=pltpu.CompilerParams(vmem_limit_bytes=24 * 2**20),
        name="first_adjoint",
    )(*in_hbm(downgoing, upgoing))


def forward_step(piece, own_ref, other_ref, rows, keep):
    total = None
    for k, field in enumerate((piece, turn(piece))):
        high, low = split(field.T)
        both = jnp.concatenate([high, low], axis=0)
        blocks = []
        for j, ref in enumerate((own_ref, other_ref)):
            down_high, down_low = split(ref[k, rows])
            keep(slice(2 * OWN * k + OWN * j, 2 * OWN * k + OWN * (j + 1)), down_high, down_low)
            wide = dot(both, down_high)
            blocks.append(wide[:128] + wide[128:] + dot(high, down_low))
        part = jnp.concatenate(blocks, axis=1)
        total = part if total is None else total + part
    return total


def normal_kernel(g_ref, own_ref, other_ref, q_ref, image_ref, high_ref, low_ref, w_ref):
    total = None
    for i in range(STEPS):
        rows = slice(i * STEP, (i + 1) * STEP)

        def keep(cols, high, low):
            high_ref[rows, cols] = high
            low_ref[rows, cols] = low

        part = forward_step(whole_rows(g_ref, i), own_ref, other_ref, rows, keep)
        total = part if total is None else total + part
    image = total.T
    image_ref[...] = image
    for rows, field in ((slice(0, 512), image), (slice(512, 1024), -turn(image))):
        w_ref[rows, :128], w_ref[rows, 128:] = split(field)
    for i in range(STEPS):
        rows = slice(i * STEP, (i + 1) * STEP)
        wide = dot(high_ref[rows], w_ref[...])
        put_rows(q_ref, i, wide[:, :128] + wide[:, 128:] + dot(low_ref[rows], w_ref[:, :128]))


def normal(g, own, other):
    return pl.pallas_call(
        normal_kernel,
        in_specs=[VMEM, VMEM, VMEM],
        out_specs=(VMEM, VMEM),
        out_shape=(pltpu.VMEM(g.shape, F32), pltpu.VMEM((2 * OWN, 128), F32)),
        scratch_shapes=[
            pltpu.VMEM((ROWS, 4 * OWN), BF16),
            pltpu.VMEM((ROWS, 4 * OWN), BF16),
            pltpu.VMEM((4 * OWN, 256), BF16),
        ],
        compiler_params=pltpu.CompilerParams(vmem_limit_bytes=28 * 2**20),
        name="normal_product",
    )(*in_vmem(g, own, other))


def second_kernel(g_ref, q_ref, own_ref, other_ref, image0_ref, keep_ref, give_ref, row_ref, p_ref):
    g, q = g_ref[...], q_ref[...]
    gamma0 = jnp.sum(g * g)
    m = jnp.sum(g * q)
    g1 = g - ratio(gamma0, m, 1.0) * q
    gamma1 = jnp.sum(g1 * g1)
    p_ref[...] = g1 + ratio(gamma1, gamma0, 0.0) * g

    total = None
    for i in range(STEPS):
        rows = slice(i * STEP, (i + 1) * STEP)
        part = forward_step(whole_rows(p_ref, i), own_ref, other_ref, rows, lambda *_: None)
        total = part if total is None else total + part
    image = total.T
    square = jnp.sum(image * image)
    lane = lax.broadcasted_iota(jnp.int32, row_ref.shape, 2)
    row_ref[...] = jnp.where(
        lane == 0, square, jnp.where(lane == 1, gamma0, jnp.where(lane == 2, m, gamma1))
    )
    near = lax.axis_index("y_low") * 4 + lax.axis_index("x")
    far, core = lax.axis_index("y_high"), lax.axis_index("core")
    own_rows = pl.ds(pl.multiple_of(core * 32, 32), 32)
    other_rows = pl.ds(pl.multiple_of((1 - core) * 32, 32), 32)
    for ref, sources, receivers in ((keep_ref, slice(0, OWN), own_rows), (give_ref, slice(OWN, 2 * OWN), other_rows)):
        ref[:OWN] = image0_ref[sources]
        ref[OWN : 2 * OWN] = image[sources]
        ref[2 * OWN : 2 * OWN + 32] = g_ref[near, far, receivers]
        ref[2 * OWN + 32 :] = p_ref[near, far, receivers]


def second_forward(g, q, own, other, image0):
    pack = pltpu.VMEM((2 * OWN + 64, 128), F32)
    return pl.pallas_call(
        second_kernel,
        in_specs=[VMEM] * 5,
        out_specs=(VMEM,) * 3,
        out_shape=(pack, pack, pltpu.VMEM((2 * CHIPS, 1, 128), F32)),
        scratch_shapes=[pltpu.VMEM(g.shape, F32)],
        compiler_params=pltpu.CompilerParams(vmem_limit_bytes=16 * 2**20),
        name="second_forward",
    )(*in_vmem(g, q, own, other, image0))


def last_kernel(got_ref, up_ref, keep_ref, take_ref, filt_ref, residual_ref):
    got = got_ref[:, 0, :]
    odd = lax.broadcasted_iota(jnp.int32, got.shape, 0) % 2 == 1
    squares = jnp.sum(jnp.where(odd, 0.0, got), axis=0, keepdims=True), jnp.sum(jnp.where(odd, got, 0.0), axis=0, keepdims=True)
    coefficient = [(squares[c][:, 0:1], got[c : c + 1, 1:2], got[c : c + 1, 2:3], got[c : c + 1, 3:4]) for c in range(2)]
    gamma = coefficient[0][1] + coefficient[1][1]
    alpha0 = gamma / (coefficient[0][2] + coefficient[1][2])
    gamma_new = 0.0
    scales = []
    for square, gamma0, m, gamma1 in coefficient:
        s = alpha0 / ratio(gamma0, m, 1.0)
        scales.append(s)
        gamma_new = gamma_new + s * s * gamma1 + (1.0 - s) * (1.0 - s) * gamma0
    beta = gamma_new / gamma
    norm = 0.0
    shifts = []
    for s, (square, gamma0, m, gamma1) in zip(scales, coefficient):
        e = beta + 1.0 - s - s * ratio(gamma1, gamma0, 0.0)
        shifts.append(e)
        norm = norm + s * s * square + e * e * m
    alpha1 = gamma_new / norm
    for_g = [alpha0 + alpha1 * e for e in shifts]
    for_p = [alpha1 * s for s in scales]

    low = lax.axis_index("core") == 0

    def both(rows):
        mine, theirs = keep_ref[rows], take_ref[rows]
        return jnp.where(low, mine, theirs), jnp.where(low, theirs, mine)

    def combine(first, second):
        columns = [for_g[c] * first[c] + for_p[c] * second[c] for c in range(2)]
        return halves(*columns)

    re, im = combine(both(slice(0, OWN)), both(slice(OWN, 2 * OWN)))
    residual_ref[0] = up_ref[0] - re
    residual_ref[1] = up_ref[1] - im
    re, im = combine(both(slice(2 * OWN, 2 * OWN + 32)), both(slice(2 * OWN + 32, 2 * OWN + 64)))
    filt_ref[:, 0, :] = re
    filt_ref[:, 1, :] = im


def last(got, upgoing, keep, take):
    return pl.pallas_call(
        last_kernel,
        in_specs=[VMEM] * 4,
        out_specs=(VMEM, VMEM),
        out_shape=(jax.ShapeDtypeStruct((32, 2, 128), F32), jax.ShapeDtypeStruct((2, OWN, 128), F32)),
        compiler_params=pltpu.CompilerParams(vmem_limit_bytes=12 * 2**20),
        name="last_update",
    )(got, upgoing, keep, take)


def small(body, shape, name, *arrays):
    return pl.pallas_call(
        body,
        in_specs=[VMEM] * len(arrays),
        out_specs=VMEM,
        out_shape=pltpu.VMEM(shape, F32),
        compiler_params=pltpu.CompilerParams(vmem_limit_bytes=4 * 2**20),
        name=name,
    )(*in_vmem(*arrays))


def add_kernel(a_ref, b_ref, out_ref):
    out_ref[...] = a_ref[...] + b_ref[...]


def total(ref):
    value = ref[0]
    for k in range(1, ref.shape[0]):
        value = value + ref[k]
    return value


def sum_kernel(ref, out_ref):
    out_ref[...] = total(ref)


def sum_repeat_kernel(ref, out_ref):
    value = total(ref)
    for k in range(out_ref.shape[0]):
        out_ref[k] = value


def repeat_kernel(ref, out_ref):
    value = ref[...]
    for k in range(out_ref.shape[0]):
        out_ref[k] = value


def exchange(blocks, axis):
    return lax.all_to_all(blocks, axis, 0, 0, tiled=True)


def all_sum(partial):
    row = small(sum_kernel, partial.shape[1:], "sum_near", exchange(partial, NEAR))
    row = small(sum_repeat_kernel, row.shape, "sum_far", exchange(row, "y_high"))
    whole = small(repeat_kernel, partial.shape, "repeat_near", exchange(row, "y_high"))
    return exchange(whole, NEAR)


def on_device(downgoing, upgoing):
    mine, theirs, down = first_adjoint(downgoing, upgoing)
    theirs = lax.ppermute(theirs, SRC, SWAP)
    down, theirs = lax.optimization_barrier((down, theirs))
    other_down = lax.ppermute(down, SRC, SWAP)
    g = all_sum(small(add_kernel, mine.shape, "add_cores", mine, theirs))
    q, image0 = normal(g, down, other_down)
    q = all_sum(q)
    keep, give, row = second_forward(g, q, down, other_down, image0)
    take = lax.ppermute(give, SRC, SWAP)
    got = lax.all_to_all(row, SRC, 0, 0, tiled=True)
    return last(got, upgoing, keep, take)


def solution(mesh):
    devices = mesh.devices.reshape(mesh.shape["freq"], 4, 2, 4, 2)
    return jax.shard_map(
        on_device,
        mesh=Mesh(devices, ("freq",) + SRC),
        in_specs=(P("freq", None, SRC), P("freq", SRC, None)),
        out_specs=(P(SRC, "freq", None), P("freq", SRC, None)),
        check_vma=False,
    )
```

```python
import jax
import jax.numpy as jnp
from jax import lax
from jax.experimental import pallas as pl
from jax.experimental.pallas import tpu as pltpu
from jax.sharding import Mesh, PartitionSpec as P

SRC = ("y_high", "y_low", "x", "core")
NEAR = ("y_low", "x")
CHIPS = 32
ROWS = 2048
OWN = 256
STEP = 512
STEPS = ROWS // STEP
SWAP = [(i, i ^ 1) for i in range(2 * CHIPS)]
VMEM = pl.BlockSpec(memory_space=pltpu.VMEM)
HBM = pl.BlockSpec(memory_space=pltpu.HBM)
F32 = jnp.float32
BF16 = jnp.bfloat16


def in_vmem(*arrays):
    return [pltpu.with_memory_space_constraint(a, pltpu.VMEM) for a in arrays]


def in_hbm(*arrays):
    return [pltpu.with_memory_space_constraint(a, pltpu.HBM) for a in arrays]


def dot(a, b):
    return jnp.dot(a, b, preferred_element_type=F32)


def split(x):
    high = x.astype(BF16)
    return high, (x - high.astype(F32)).astype(BF16)


def lanes(x):
    return lax.broadcasted_iota(jnp.int32, x.shape, x.ndim - 1) < 64


def turn(z):
    swapped = pltpu.roll(z, 64, 1)
    return jnp.where(lanes(z), -swapped, swapped)


def halves(re, im):
    first = lanes(re)
    return jnp.where(first, re, pltpu.roll(im, 64, 1)), jnp.where(first, pltpu.roll(re, 64, 1), im)


def ratio(a, b, other):
    good = b > 0
    return jnp.where(good, a / jnp.where(good, b, 1.0), other)


def whole_rows(ref, i):
    return ref[:, i].reshape(STEP, 128)


def put_rows(ref, i, value):
    ref[:, i] = value.reshape(8, 64, 128)


def first_kernel(down_hbm, up_hbm, mine_ref, theirs_ref, down_ref, up_ref, high_ref, low_ref, sem):
    field_copy = pltpu.make_async_copy(up_hbm, up_ref, sem.at[0])
    field_copy.start()
    down_copy = pltpu.make_async_copy(down_hbm, down_ref, sem.at[1])
    down_copy.start()
    field_copy.wait()
    lower, upper = halves(up_ref[0], up_ref[1])
    swap = lax.axis_index("core") == 1
    for k, half in enumerate((jnp.where(swap, upper, lower), jnp.where(swap, lower, upper))):
        cols = slice(128 * k, 128 * k + 128)
        for rows, field in ((slice(0, OWN), half), (slice(OWN, 2 * OWN), -turn(half))):
            high_ref[rows, cols], low_ref[rows, cols] = split(field)
    down_copy.wait()
    parts = [split(down_ref[k]) for k in range(2)]
    high = jnp.concatenate([parts[0][0], parts[1][0]], axis=1)
    low = jnp.concatenate([parts[0][1], parts[1][1]], axis=1)
    total = dot(high, high_ref[...]) + dot(high, low_ref[...]) + dot(low, high_ref[...])
    for i in range(STEPS):
        rows = slice(i * STEP, (i + 1) * STEP)
        put_rows(mine_ref, i, total[rows, :128])
        put_rows(theirs_ref, i, total[rows, 128:])


def first_adjoint(downgoing, upgoing):
    out = pltpu.VMEM((8, 4, 64, 128), F32)
    return pl.pallas_call(
        first_kernel,
        in_specs=[HBM, HBM],
        out_specs=(VMEM, VMEM, VMEM),
        out_shape=(out, out, pltpu.VMEM(downgoing.shape, F32)),
        scratch_shapes=[
            pltpu.VMEM(upgoing.shape, F32),
            pltpu.VMEM((2 * OWN, 256), BF16),
            pltpu.VMEM((2 * OWN, 256), BF16),
            pltpu.SemaphoreType.DMA((2,)),
        ],
        compiler_params=pltpu.CompilerParams(vmem_limit_bytes=24 * 2**20),
        name="first_adjoint",
    )(*in_hbm(downgoing, upgoing))


def forward_step(piece, own_ref, other_ref, rows, keep):
    total = None
    for k, field in enumerate((piece, turn(piece))):
        high, low = split(field.T)
        both = jnp.concatenate([high, low], axis=0)
        blocks = []
        for j, ref in enumerate((own_ref, other_ref)):
            down_high, down_low = split(ref[k, rows])
            keep(slice(2 * OWN * k + OWN * j, 2 * OWN * k + OWN * (j + 1)), down_high, down_low)
            wide = dot(both, down_high)
            blocks.append(wide[:128] + wide[128:] + dot(high, down_low))
        part = jnp.concatenate(blocks, axis=1)
        total = part if total is None else total + part
    return total


def normal_kernel(g_ref, own_ref, other_ref, q_ref, image_ref, high_ref, low_ref, w_ref):
    total = None
    for i in range(STEPS):
        rows = slice(i * STEP, (i + 1) * STEP)

        def keep(cols, high, low):
            high_ref[rows, cols] = high
            low_ref[rows, cols] = low

        part = forward_step(whole_rows(g_ref, i), own_ref, other_ref, rows, keep)
        total = part if total is None else total + part
    image = total.T
    image_ref[...] = image
    for rows, field in ((slice(0, 512), image), (slice(512, 1024), -turn(image))):
        w_ref[rows, :128], w_ref[rows, 128:] = split(field)
    for i in range(STEPS):
        rows = slice(i * STEP, (i + 1) * STEP)
        wide = dot(high_ref[rows], w_ref[...])
        put_rows(q_ref, i, wide[:, :128] + wide[:, 128:] + dot(low_ref[rows], w_ref[:, :128]))


def normal(g, own, other):
    return pl.pallas_call(
        normal_kernel,
        in_specs=[VMEM, VMEM, VMEM],
        out_specs=(VMEM, VMEM),
        out_shape=(pltpu.VMEM(g.shape, F32), pltpu.VMEM((2 * OWN, 128), F32)),
        scratch_shapes=[
            pltpu.VMEM((ROWS, 4 * OWN), BF16),
            pltpu.VMEM((ROWS, 4 * OWN), BF16),
            pltpu.VMEM((4 * OWN, 256), BF16),
        ],
        compiler_params=pltpu.CompilerParams(vmem_limit_bytes=28 * 2**20),
        name="normal_product",
    )(*in_vmem(g, own, other))


def second_kernel(g_ref, q_ref, own_ref, other_ref, image0_ref, keep_ref, give_ref, row_ref, p_ref):
    g, q = g_ref[...], q_ref[...]
    gamma0 = jnp.sum(g * g)
    m = jnp.sum(g * q)
    g1 = g - ratio(gamma0, m, 1.0) * q
    gamma1 = jnp.sum(g1 * g1)
    p_ref[...] = g1 + ratio(gamma1, gamma0, 0.0) * g

    total = None
    for i in range(STEPS):
        rows = slice(i * STEP, (i + 1) * STEP)
        part = forward_step(whole_rows(p_ref, i), own_ref, other_ref, rows, lambda *_: None)
        total = part if total is None else total + part
    image = total.T
    square = jnp.sum(image * image)
    lane = lax.broadcasted_iota(jnp.int32, row_ref.shape, 2)
    row_ref[...] = jnp.where(
        lane == 0, square, jnp.where(lane == 1, gamma0, jnp.where(lane == 2, m, gamma1))
    )
    near = lax.axis_index("y_low") * 4 + lax.axis_index("x")
    far, core = lax.axis_index("y_high"), lax.axis_index("core")
    own_rows = pl.ds(pl.multiple_of(core * 32, 32), 32)
    other_rows = pl.ds(pl.multiple_of((1 - core) * 32, 32), 32)
    for ref, sources, receivers in ((keep_ref, slice(0, OWN), own_rows), (give_ref, slice(OWN, 2 * OWN), other_rows)):
        ref[:OWN] = image0_ref[sources]
        ref[OWN : 2 * OWN] = image[sources]
        ref[2 * OWN : 2 * OWN + 32] = g_ref[near, far, receivers]
        ref[2 * OWN + 32 :] = p_ref[near, far, receivers]


def second_forward(g, q, own, other, image0):
    pack = pltpu.VMEM((2 * OWN + 64, 128), F32)
    return pl.pallas_call(
        second_kernel,
        in_specs=[VMEM] * 5,
        out_specs=(VMEM,) * 3,
        out_shape=(pack, pack, pltpu.VMEM((2 * CHIPS, 1, 128), F32)),
        scratch_shapes=[pltpu.VMEM(g.shape, F32)],
        compiler_params=pltpu.CompilerParams(vmem_limit_bytes=16 * 2**20),
        name="second_forward",
    )(*in_vmem(g, q, own, other, image0))


def last_kernel(got_ref, up_ref, keep_ref, take_ref, filt_ref, residual_ref):
    got = got_ref[:, 0, :]
    odd = lax.broadcasted_iota(jnp.int32, got.shape, 0) % 2 == 1
    squares = jnp.sum(jnp.where(odd, 0.0, got), axis=0, keepdims=True), jnp.sum(jnp.where(odd, got, 0.0), axis=0, keepdims=True)
    coefficient = [(squares[c][:, 0:1], got[c : c + 1, 1:2], got[c : c + 1, 2:3], got[c : c + 1, 3:4]) for c in range(2)]
    gamma = coefficient[0][1] + coefficient[1][1]
    alpha0 = gamma / (coefficient[0][2] + coefficient[1][2])
    gamma_new = 0.0
    scales = []
    for square, gamma0, m, gamma1 in coefficient:
        s = alpha0 / ratio(gamma0, m, 1.0)
        scales.append(s)
        gamma_new = gamma_new + s * s * gamma1 + (1.0 - s) * (1.0 - s) * gamma0
    beta = gamma_new / gamma
    norm = 0.0
    shifts = []
    for s, (square, gamma0, m, gamma1) in zip(scales, coefficient):
        e = beta + 1.0 - s - s * ratio(gamma1, gamma0, 0.0)
        shifts.append(e)
        norm = norm + s * s * square + e * e * m
    alpha1 = gamma_new / norm
    for_g = [alpha0 + alpha1 * e for e in shifts]
    for_p = [alpha1 * s for s in scales]

    low = lax.axis_index("core") == 0

    def both(rows):
        mine, theirs = keep_ref[rows], take_ref[rows]
        return jnp.where(low, mine, theirs), jnp.where(low, theirs, mine)

    def combine(first, second):
        columns = [for_g[c] * first[c] + for_p[c] * second[c] for c in range(2)]
        return halves(*columns)

    re, im = combine(both(slice(0, OWN)), both(slice(OWN, 2 * OWN)))
    residual_ref[0] = up_ref[0] - re
    residual_ref[1] = up_ref[1] - im
    re, im = combine(both(slice(2 * OWN, 2 * OWN + 32)), both(slice(2 * OWN + 32, 2 * OWN + 64)))
    filt_ref[:, 0, :] = re
    filt_ref[:, 1, :] = im


def last(got, upgoing, keep, take):
    return pl.pallas_call(
        last_kernel,
        in_specs=[VMEM] * 4,
        out_specs=(VMEM, VMEM),
        out_shape=(jax.ShapeDtypeStruct((32, 2, 128), F32), jax.ShapeDtypeStruct((2, OWN, 128), F32)),
        compiler_params=pltpu.CompilerParams(vmem_limit_bytes=12 * 2**20),
        name="last_update",
    )(got, upgoing, keep, take)


def small(body, shape, name, *arrays):
    return pl.pallas_call(
        body,
        in_specs=[VMEM] * len(arrays),
        out_specs=VMEM,
        out_shape=pltpu.VMEM(shape, F32),
        compiler_params=pltpu.CompilerParams(vmem_limit_bytes=4 * 2**20),
        name=name,
    )(*in_vmem(*arrays))


def add_kernel(a_ref, b_ref, out_ref):
    out_ref[...] = a_ref[...] + b_ref[...]


def total(ref):
    value = ref[0]
    for k in range(1, ref.shape[0]):
        value = value + ref[k]
    return value


def sum_kernel(ref, out_ref):
    out_ref[...] = total(ref)


def sum_repeat_kernel(ref, out_ref):
    value = total(ref)
    for k in range(out_ref.shape[0]):
        out_ref[k] = value


def repeat_kernel(ref, out_ref):
    value = ref[...]
    for k in range(out_ref.shape[0]):
        out_ref[k] = value


def exchange(blocks, axis):
    return lax.all_to_all(blocks, axis, 0, 0, tiled=True)


def far_one_step(row):
    rows = small(repeat_kernel, (4,) + row.shape, "repeat_far", row)
    return small(sum_kernel, row.shape, "sum_far", exchange(rows, "y_high"))


def far_two_steps(row):
    block = small(sum_repeat_kernel, row.shape, "sum_far", exchange(row, "y_high"))
    return exchange(block, "y_high")


def all_sum(partial, far):
    row = far(small(sum_kernel, partial.shape[1:], "sum_near", exchange(partial, NEAR)))
    return exchange(small(repeat_kernel, partial.shape, "repeat_near", row), NEAR)


def on_device(downgoing, upgoing):
    mine, theirs, down = first_adjoint(downgoing, upgoing)
    theirs = lax.ppermute(theirs, SRC, SWAP)
    down, theirs = lax.optimization_barrier((down, theirs))
    other_down = lax.ppermute(down, SRC, SWAP)
    g = all_sum(small(add_kernel, mine.shape, "add_cores", mine, theirs), far_two_steps)
    q, image0 = normal(g, down, other_down)
    q = all_sum(q, far_one_step)
    keep, give, row = second_forward(g, q, down, other_down, image0)
    take = lax.ppermute(give, SRC, SWAP)
    got = lax.all_to_all(row, SRC, 0, 0, tiled=True)
    return last(got, upgoing, keep, take)


def solution(mesh):
    devices = mesh.devices.reshape(mesh.shape["freq"], 4, 2, 4, 2)
    return jax.shard_map(
        on_device,
        mesh=Mesh(devices, ("freq",) + SRC),
        in_specs=(P("freq", None, SRC), P("freq", SRC, None)),
        out_specs=(P(SRC, "freq", None), P("freq", SRC, None)),
        check_vma=False,
    )
```

```python
import jax
import jax.numpy as jnp
from jax import lax
from jax.experimental import pallas as pl
from jax.experimental.pallas import tpu as pltpu
from jax.sharding import Mesh, PartitionSpec as P

SRC = ("y_high", "y_low", "x", "core")
NEAR = ("y_low", "x")
CHIPS = 32
ROWS = 2048
OWN = 256
STEP = 512
STEPS = ROWS // STEP
SWAP = [(i, i ^ 1) for i in range(2 * CHIPS)]
VMEM = pl.BlockSpec(memory_space=pltpu.VMEM)
HBM = pl.BlockSpec(memory_space=pltpu.HBM)
F32 = jnp.float32
BF16 = jnp.bfloat16


def in_vmem(*arrays):
    return [pltpu.with_memory_space_constraint(a, pltpu.VMEM) for a in arrays]


def in_hbm(*arrays):
    return [pltpu.with_memory_space_constraint(a, pltpu.HBM) for a in arrays]


def dot(a, b):
    return jnp.dot(a, b, preferred_element_type=F32)


def split(x):
    high = x.astype(BF16)
    return high, (x - high.astype(F32)).astype(BF16)


def lanes(x):
    return lax.broadcasted_iota(jnp.int32, x.shape, x.ndim - 1) < 64


def turn(z):
    swapped = pltpu.roll(z, 64, 1)
    return jnp.where(lanes(z), -swapped, swapped)


def halves(re, im):
    first = lanes(re)
    return jnp.where(first, re, pltpu.roll(im, 64, 1)), jnp.where(first, pltpu.roll(re, 64, 1), im)


def ratio(a, b, other):
    good = b > 0
    return jnp.where(good, a / jnp.where(good, b, 1.0), other)


def whole_rows(ref, i):
    return ref[:, i].reshape(STEP, 128)


def put_rows(ref, i, value):
    ref[:, i] = value.reshape(8, 64, 128)


def first_kernel(down_hbm, up_hbm, mine_ref, theirs_ref, down_ref, up_ref, high_ref, low_ref, sem):
    field_copy = pltpu.make_async_copy(up_hbm, up_ref, sem.at[0])
    field_copy.start()
    down_copy = pltpu.make_async_copy(down_hbm, down_ref, sem.at[1])
    down_copy.start()
    field_copy.wait()
    lower, upper = halves(up_ref[0], up_ref[1])
    swap = lax.axis_index("core") == 1
    for k, half in enumerate((jnp.where(swap, upper, lower), jnp.where(swap, lower, upper))):
        cols = slice(128 * k, 128 * k + 128)
        for rows, field in ((slice(0, OWN), half), (slice(OWN, 2 * OWN), -turn(half))):
            high_ref[rows, cols], low_ref[rows, cols] = split(field)
    down_copy.wait()
    parts = [split(down_ref[k]) for k in range(2)]
    high = jnp.concatenate([parts[0][0], parts[1][0]], axis=1)
    low = jnp.concatenate([parts[0][1], parts[1][1]], axis=1)
    total = dot(high, high_ref[...]) + dot(high, low_ref[...]) + dot(low, high_ref[...])
    for i in range(STEPS):
        rows = slice(i * STEP, (i + 1) * STEP)
        put_rows(mine_ref, i, total[rows, :128])
        put_rows(theirs_ref, i, total[rows, 128:])


def first_adjoint(downgoing, upgoing):
    out = pltpu.VMEM((8, 4, 64, 128), F32)
    return pl.pallas_call(
        first_kernel,
        in_specs=[HBM, HBM],
        out_specs=(VMEM, VMEM, VMEM),
        out_shape=(out, out, pltpu.VMEM(downgoing.shape, F32)),
        scratch_shapes=[
            pltpu.VMEM(upgoing.shape, F32),
            pltpu.VMEM((2 * OWN, 256), BF16),
            pltpu.VMEM((2 * OWN, 256), BF16),
            pltpu.SemaphoreType.DMA((2,)),
        ],
        compiler_params=pltpu.CompilerParams(vmem_limit_bytes=24 * 2**20),
        name="first_adjoint",
    )(*in_hbm(downgoing, upgoing))


def forward_step(piece, own_ref, other_ref, rows, keep):
    total = None
    for k, field in enumerate((piece, turn(piece))):
        high, low = split(field.T)
        both = jnp.concatenate([high, low], axis=0)
        blocks = []
        for j, ref in enumerate((own_ref, other_ref)):
            down_high, down_low = split(ref[k, rows])
            keep(slice(2 * OWN * k + OWN * j, 2 * OWN * k + OWN * (j + 1)), down_high, down_low)
            wide = dot(both, down_high)
            blocks.append(wide[:128] + wide[128:] + dot(high, down_low))
        part = jnp.concatenate(blocks, axis=1)
        total = part if total is None else total + part
    return total


def normal_kernel(g_ref, own_ref, other_ref, q_ref, image_ref, high_ref, low_ref, w_ref):
    total = None
    for i in range(STEPS):
        rows = slice(i * STEP, (i + 1) * STEP)

        def keep(cols, high, low):
            high_ref[rows, cols] = high
            low_ref[rows, cols] = low

        part = forward_step(whole_rows(g_ref, i), own_ref, other_ref, rows, keep)
        total = part if total is None else total + part
    image = total.T
    image_ref[...] = image
    for rows, field in ((slice(0, 512), image), (slice(512, 1024), -turn(image))):
        w_ref[rows, :128], w_ref[rows, 128:] = split(field)
    for i in range(STEPS):
        rows = slice(i * STEP, (i + 1) * STEP)
        wide = dot(high_ref[rows], w_ref[...])
        put_rows(q_ref, i, wide[:, :128] + wide[:, 128:] + dot(low_ref[rows], w_ref[:, :128]))


def normal(g, own, other):
    return pl.pallas_call(
        normal_kernel,
        in_specs=[VMEM, VMEM, VMEM],
        out_specs=(VMEM, VMEM),
        out_shape=(pltpu.VMEM(g.shape, F32), pltpu.VMEM((2 * OWN, 128), F32)),
        scratch_shapes=[
            pltpu.VMEM((ROWS, 4 * OWN), BF16),
            pltpu.VMEM((ROWS, 4 * OWN), BF16),
            pltpu.VMEM((4 * OWN, 256), BF16),
        ],
        compiler_params=pltpu.CompilerParams(vmem_limit_bytes=28 * 2**20),
        name="normal_product",
    )(*in_vmem(g, own, other))


def second_kernel(g_ref, q_ref, own_ref, other_ref, image0_ref, keep_ref, give_ref, row_ref, p_ref):
    g, q = g_ref[...], q_ref[...]
    gamma0 = jnp.sum(g * g)
    m = jnp.sum(g * q)
    g1 = g - ratio(gamma0, m, 1.0) * q
    gamma1 = jnp.sum(g1 * g1)
    p_ref[...] = g1 + ratio(gamma1, gamma0, 0.0) * g

    total = None
    for i in range(STEPS):
        rows = slice(i * STEP, (i + 1) * STEP)
        part = forward_step(whole_rows(p_ref, i), own_ref, other_ref, rows, lambda *_: None)
        total = part if total is None else total + part
    image = total.T
    square = jnp.sum(image * image)
    lane = lax.broadcasted_iota(jnp.int32, row_ref.shape, 2)
    row_ref[...] = jnp.where(
        lane == 0, square, jnp.where(lane == 1, gamma0, jnp.where(lane == 2, m, gamma1))
    )
    near = lax.axis_index("y_low") * 4 + lax.axis_index("x")
    far, core = lax.axis_index("y_high"), lax.axis_index("core")
    own_rows = pl.ds(pl.multiple_of(core * 32, 32), 32)
    other_rows = pl.ds(pl.multiple_of((1 - core) * 32, 32), 32)
    for ref, sources, receivers in ((keep_ref, slice(0, OWN), own_rows), (give_ref, slice(OWN, 2 * OWN), other_rows)):
        ref[:OWN] = image0_ref[sources]
        ref[OWN : 2 * OWN] = image[sources]
        ref[2 * OWN : 2 * OWN + 32] = g_ref[near, far, receivers]
        ref[2 * OWN + 32 :] = p_ref[near, far, receivers]


def second_forward(g, q, own, other, image0):
    pack = pltpu.VMEM((2 * OWN + 64, 128), F32)
    return pl.pallas_call(
        second_kernel,
        in_specs=[VMEM] * 5,
        out_specs=(VMEM,) * 3,
        out_shape=(pack, pack, pltpu.VMEM((2 * CHIPS, 1, 128), F32)),
        scratch_shapes=[pltpu.VMEM(g.shape, F32)],
        compiler_params=pltpu.CompilerParams(vmem_limit_bytes=16 * 2**20),
        name="second_forward",
    )(*in_vmem(g, q, own, other, image0))


def last_kernel(got_ref, up_ref, keep_ref, take_ref, filt_ref, residual_ref):
    got = got_ref[:, 0, :]
    odd = lax.broadcasted_iota(jnp.int32, got.shape, 0) % 2 == 1
    squares = jnp.sum(jnp.where(odd, 0.0, got), axis=0, keepdims=True), jnp.sum(jnp.where(odd, got, 0.0), axis=0, keepdims=True)
    coefficient = [(squares[c][:, 0:1], got[c : c + 1, 1:2], got[c : c + 1, 2:3], got[c : c + 1, 3:4]) for c in range(2)]
    gamma = coefficient[0][1] + coefficient[1][1]
    alpha0 = gamma / (coefficient[0][2] + coefficient[1][2])
    gamma_new = 0.0
    scales = []
    for square, gamma0, m, gamma1 in coefficient:
        s = alpha0 / ratio(gamma0, m, 1.0)
        scales.append(s)
        gamma_new = gamma_new + s * s * gamma1 + (1.0 - s) * (1.0 - s) * gamma0
    beta = gamma_new / gamma
    norm = 0.0
    shifts = []
    for s, (square, gamma0, m, gamma1) in zip(scales, coefficient):
        e = beta + 1.0 - s - s * ratio(gamma1, gamma0, 0.0)
        shifts.append(e)
        norm = norm + s * s * square + e * e * m
    alpha1 = gamma_new / norm
    for_g = [alpha0 + alpha1 * e for e in shifts]
    for_p = [alpha1 * s for s in scales]

    low = lax.axis_index("core") == 0

    def both(rows):
        mine, theirs = keep_ref[rows], take_ref[rows]
        return jnp.where(low, mine, theirs), jnp.where(low, theirs, mine)

    def combine(first, second):
        columns = [for_g[c] * first[c] + for_p[c] * second[c] for c in range(2)]
        return halves(*columns)

    re, im = combine(both(slice(0, OWN)), both(slice(OWN, 2 * OWN)))
    residual_ref[0] = up_ref[0] - re
    residual_ref[1] = up_ref[1] - im
    re, im = combine(both(slice(2 * OWN, 2 * OWN + 32)), both(slice(2 * OWN + 32, 2 * OWN + 64)))
    filt_ref[:, 0, :] = re
    filt_ref[:, 1, :] = im


def last(got, upgoing, keep, take):
    return pl.pallas_call(
        last_kernel,
        in_specs=[VMEM] * 4,
        out_specs=(VMEM, VMEM),
        out_shape=(jax.ShapeDtypeStruct((32, 2, 128), F32), jax.ShapeDtypeStruct((2, OWN, 128), F32)),
        compiler_params=pltpu.CompilerParams(vmem_limit_bytes=12 * 2**20),
        name="last_update",
    )(got, upgoing, keep, take)


def small(body, shape, name, *arrays):
    return pl.pallas_call(
        body,
        in_specs=[VMEM] * len(arrays),
        out_specs=VMEM,
        out_shape=pltpu.VMEM(shape, F32),
        compiler_params=pltpu.CompilerParams(vmem_limit_bytes=4 * 2**20),
        name=name,
    )(*in_vmem(*arrays))


def add_kernel(a_ref, b_ref, out_ref):
    out_ref[...] = a_ref[...] + b_ref[...]


def total(ref):
    value = ref[0]
    for k in range(1, ref.shape[0]):
        value = value + ref[k]
    return value


def sum_kernel(ref, out_ref):
    out_ref[...] = total(ref)


def sum_repeat_kernel(ref, out_ref):
    value = total(ref)
    for k in range(out_ref.shape[0]):
        out_ref[k] = value


def repeat_kernel(ref, out_ref):
    value = ref[...]
    for k in range(out_ref.shape[0]):
        out_ref[k] = value


def exchange(blocks, axis):
    return lax.all_to_all(blocks, axis, 0, 0, tiled=True)


def far_one_step(row):
    rows = small(repeat_kernel, (4,) + row.shape, "repeat_far", row)
    return small(sum_kernel, row.shape, "sum_far", exchange(rows, "y_high"))


def far_two_steps(row):
    block = small(sum_repeat_kernel, row.shape, "sum_far", exchange(row, "y_high"))
    return exchange(block, "y_high")


def all_sum(partial, far):
    row = far(small(sum_kernel, partial.shape[1:], "sum_near", exchange(partial, NEAR)))
    return exchange(small(repeat_kernel, partial.shape, "repeat_near", row), NEAR)


def on_device(downgoing, upgoing):
    mine, theirs, down = first_adjoint(downgoing, upgoing)
    other_down = lax.ppermute(down, SRC, SWAP)
    theirs = lax.ppermute(theirs, SRC, SWAP)
    g = all_sum(small(add_kernel, mine.shape, "add_cores", mine, theirs), far_two_steps)
    g, down = lax.optimization_barrier((g, down))
    q, image0 = normal(g, down, other_down)
    q = all_sum(q, far_one_step)
    keep, give, row = second_forward(g, q, down, other_down, image0)
    take = lax.ppermute(give, SRC, SWAP)
    got = lax.all_to_all(row, SRC, 0, 0, tiled=True)
    return last(got, upgoing, keep, take)


def solution(mesh):
    devices = mesh.devices.reshape(mesh.shape["freq"], 4, 2, 4, 2)
    return jax.shard_map(
        on_device,
        mesh=Mesh(devices, ("freq",) + SRC),
        in_specs=(P("freq", None, SRC), P("freq", SRC, None)),
        out_specs=(P(SRC, "freq", None), P("freq", SRC, None)),
        check_vma=False,
    )
```
